128 devices in a mesh: wide: 16 (over y, x_lo, core), narrow: 8 (over x_hi, z).
Axes of the slice: x: 4 (x_hi: 2, x_lo: 2; x = x_hi * 2 + x_lo), y: 4, z: 4, core: 2. Of those that a mesh axis runs over, the one named last changes fastest.
Arguments:
- inputs: bfloat16 [1024, 8192], P('wide', 'narrow'), may hold values from -6 to 6
- grad_out: bfloat16 [1024, 8192], P('wide', 'narrow'), may hold values from -6 to 6
- w_gate: bfloat16 [8192, 29568], P('narrow', 'wide'), may hold values from -0.0625 to 0.0625
- w_up: bfloat16 [8192, 29568], P('narrow', 'wide'), may hold values from -0.0625 to 0.0625
- w_down: bfloat16 [29568, 8192], P('wide', 'narrow'), may hold values from -0.03125 to 0.03125
Outputs:
- grad_input: bfloat16 [1024, 8192], P('wide', 'narrow')
- grad_gate: bfloat16 [8192, 29568], P('narrow', 'wide')
- grad_up: bfloat16 [8192, 29568], P('narrow', 'wide')
- grad_down: bfloat16 [29568, 8192], P('wide', 'narrow')
The draws below stay inside these ranges and needn't reach their ends.
All inputs are finite; a program needn't handle non-finite values.
Results may differ from the reference program's by a relative error of at most 0.033.
Values may be sent and summed in bfloat16 or wider, within the bound.
No kernel may reach another device: no remote copies, remote signals or barrier semaphores. Data moves between devices by JAX's collectives and lax.ppermute only.
A program may use at most 128 MiB of HBM per device.

```python
import jax
import jax.numpy as jnp
from jax import lax

D = 8192
FF = 29568
TOKENS = 1024
N_NARROW = 8


def level_of(key, dims, split, least, top_value):
    loudness = 1.0
    for dim, parts in split:
        draws = jax.random.uniform(jax.random.fold_in(jax.random.fold_in(key, 6), dim), (parts,), jnp.float32, least / len(split), top_value / len(split))
        loudness = loudness * jnp.repeat(jnp.exp(draws), dims[dim] // parts).reshape((-1,) + (1,) * (len(dims) - 1 - dim))
    return loudness


def gaussian(own_key, extent, spread, bound, cuts=(), dtype=jnp.bfloat16):
    result = spread * jax.random.normal(own_key, extent, jnp.float32)
    if cuts:
        result = result * level_of(own_key, extent, cuts, -0.22, 0.18)
    return jnp.clip(result, -bound, bound).astype(dtype)


def setup_inputs(seed: int = 0) -> dict:
    streams_of = jax.random.split(jax.random.key(seed), 6)
    inputs = gaussian(streams_of[0], (TOKENS, D), 1.0, 6.0, ((0, 16), (1, 8)))
    grad_out = gaussian(streams_of[1], (TOKENS, D), 1.0, 6.0, ((0, 16), (1, 8)))
    w_gate = gaussian(streams_of[2], (D, FF), D ** -0.5, 0.0625, ((0, 8), (1, 16)))
    w_up = gaussian(streams_of[3], (D, FF), D ** -0.5, 0.0625, ((0, 8), (1, 16)))
    w_down = gaussian(streams_of[4], (FF, D), FF ** -0.5, 0.03125, ((0, 16), (1, 8)))
    return dict(inputs=inputs, grad_out=grad_out, w_gate=w_gate, w_up=w_up, w_down=w_down)


def rounded(value):
    return lax.optimization_barrier(value.astype(jnp.bfloat16)).astype(jnp.float32)


def reference(inputs, grad_out, w_gate, w_up, w_down):
    block_width = D // N_NARROW
    gate_sum = jnp.zeros((TOKENS, FF), jnp.float32)
    up_sum = jnp.zeros((TOKENS, FF), jnp.float32)
    hidden_grad = jnp.zeros((TOKENS, FF), jnp.float32)
    for block in range(N_NARROW):
        first = block * block_width
        input_block = inputs[:, first:first + block_width]
        grad_block = grad_out[:, first:first + block_width]
        gate_sum = gate_sum + rounded(jnp.dot(input_block, w_gate[first:first + block_width], preferred_element_type=jnp.float32))
        up_sum = up_sum + rounded(jnp.dot(input_block, w_up[first:first + block_width], preferred_element_type=jnp.float32))
        hidden_grad = hidden_grad + rounded(jnp.dot(grad_block, w_down[:, first:first + block_width].T, preferred_element_type=jnp.float32))
    sigmoid_gate = jax.nn.sigmoid(gate_sum)
    hidden = (gate_sum * sigmoid_gate * up_sum).astype(jnp.bfloat16)
    gate_grad = (hidden_grad * up_sum * sigmoid_gate * (1.0 + gate_sum * (1.0 - sigmoid_gate))).astype(jnp.bfloat16)
    up_grad = (hidden_grad * gate_sum * sigmoid_gate).astype(jnp.bfloat16)
    grad_input = jnp.dot(gate_grad, w_gate.T, preferred_element_type=jnp.float32) + jnp.dot(up_grad, w_up.T, preferred_element_type=jnp.float32)
    grad_gate = jnp.dot(inputs.T, gate_grad, preferred_element_type=jnp.float32)
    grad_up = jnp.dot(inputs.T, up_grad, preferred_element_type=jnp.float32)
    grad_down = jnp.dot(hidden.T, grad_out, preferred_element_type=jnp.float32)
    return (grad_input.astype(jnp.bfloat16), grad_gate.astype(jnp.bfloat16), grad_up.astype(jnp.bfloat16), grad_down.astype(jnp.bfloat16))
```

```python
import functools

import jax
import jax.numpy as jnp
from jax import lax
from jax.experimental import pallas as pl
from jax.experimental.pallas import tpu as pltpu
from jax.sharding import PartitionSpec as P

BF = jnp.bfloat16
F32 = jnp.float32
D = 1024
T = 1024
HALF = T // 2
B = 128
FF = 1848
R = 464
Q = 4
N_BLOCK = 256
VMEM = 48 * 1024 * 1024

NT = (((1,), (1,)), ((), ()))
NN = (((1,), (0,)), ((), ()))
TN = (((0,), (0,)), ((), ()))


def dot(a, b, dims):
    return lax.dot_general(a, b, dims, preferred_element_type=F32)


def shape(*dims, dtype=BF):
    return jax.ShapeDtypeStruct(dims, dtype)


def params():
    return pltpu.CompilerParams(vmem_limit_bytes=VMEM)


def cost(flops, nbytes):
    return pl.CostEstimate(flops=int(flops), bytes_accessed=int(nbytes), transcendentals=0)


def narrow_move(value, dxh, dz):
    pairs = [
        (xh * 4 + z, ((xh + dxh) % 2) * 4 + (z + dz) % 4) for xh in range(2) for z in range(4)
    ]
    return lax.ppermute(value, "narrow", pairs)


def wide_move(value, dy, dxl, dc):
    pairs = [
        (y * 4 + xl * 2 + c, ((y + dy) % 4) * 4 + ((xl + dxl) % 2) * 2 + (c + dc) % 2)
        for y in range(4)
        for xl in range(2)
        for c in range(2)
    ]
    return lax.ppermute(value, "wide", pairs)


def first_kernel(is_x, at, xo, xt, go, gt, wg, wu, wd, *rest):
    outs, (xs, gs) = rest[:-2], rest[-2:]
    step = pl.program_id(0)
    xh = at[0]
    own = pl.multiple_of(xh * B, B)
    other = pl.multiple_of((1 - xh) * B, B)
    xs[pl.ds(own, B), :] = xo[0]
    xs[pl.ds(other, B), :] = xt[0]
    gs[pl.ds(own, B), :] = go[0]
    gs[pl.ds(other, B), :] = gt[0]
    for i, (w, src) in enumerate(((wg, xs), (wu, xs), (wd, gs))):
        res = dot(w[...], src[...], NT).astype(BF)
        near, far = res[:, :B], res[:, B:]
        if is_x:
            send, keep = outs
            keep[0, i] = near
            send[0, i] = far
        else:
            own_out, mid1, mid3, a2, b2 = outs
            for k, out in ((0, own_out), (1, mid1), (3, mid3)):

                @pl.when(step == k)
                def _(out=out):
                    out[0, i] = near
                    out[1, i] = far

            @pl.when(step == 2)
            def _():
                a2[i] = near
                b2[i] = far


def first(q, is_x, at, xg_o, xg_t, wg, wu, wd):
    def tokens(which):
        return pl.BlockSpec((1, B, D), lambda s, at: (which, lax.rem(at[1] + s, 4), 0))

    weight = pl.BlockSpec((R, D), lambda s, at: (q, 0))
    if is_x:
        out_shape = [shape(4, 3, R, B)] * 2
        out_specs = [pl.BlockSpec((1, 3, R, B), lambda s, at: (s, 0, 0, 0))] * 2
    else:
        out_shape = [shape(2, 3, R, B)] * 3 + [shape(3, R, B)] * 2
        out_specs = [pl.BlockSpec((2, 3, R, B), lambda s, at: (0, 0, 0, 0))] * 3 + [
            pl.BlockSpec((3, R, B), lambda s, at: (0, 0, 0))
        ] * 2
    return pl.pallas_call(
        functools.partial(first_kernel, is_x),
        out_shape=out_shape,
        grid_spec=pltpu.PrefetchScalarGridSpec(
            num_scalar_prefetch=1,
            grid=(4,),
            in_specs=[tokens(0), tokens(0), tokens(1), tokens(1), weight, weight, weight],
            out_specs=out_specs,
            scratch_shapes=[pltpu.VMEM((2 * B, D), BF)] * 2,
        ),
        compiler_params=params(),
        cost_estimate=cost(3 * 2 * R * T * D, 3 * R * D * 2 + 4 * T * D + 3 * R * T * 2),
        name=f"first{q}",
    )(at, xg_o, xg_t, xg_o, xg_t, wg, wu, wd)


def x_sum_kernel(keep, recv, s1, s2, s3):
    for k, out in ((1, s1), (2, s2), (3, s3)):
        out[0] = (keep[k, 0].astype(F32) + recv[k, 0].astype(F32)).astype(BF)


def x_sum(keep, recv):
    block = pl.BlockSpec((4, 1, R, B), lambda i: (0, i, 0, 0))
    return pl.pallas_call(
        x_sum_kernel,
        out_shape=[shape(3, R, B)] * 3,
        grid=(3,),
        in_specs=[block] * 2,
        out_specs=[pl.BlockSpec((1, R, B), lambda i: (i, 0, 0))] * 3,
        compiler_params=params(),
        cost_estimate=cost(3 * 3 * R * B, 11 * 3 * R * B * 2),
        name="x_sum",
    )(keep, recv)


def z_mid_kernel(mid1, ra, mid3, rb, out1, out3):
    out1[0, 0] = (mid1[0, 0].astype(F32) + ra[0].astype(F32)).astype(BF)
    out3[0, 0] = (mid3[0, 0].astype(F32) + rb[0].astype(F32)).astype(BF)


def z_mid(mid1, ra, mid3, rb):
    first_half = pl.BlockSpec((1, 1, R, B), lambda i: (0, i, 0, 0))
    second_half = pl.BlockSpec((1, 1, R, B), lambda i: (1, i, 0, 0))
    one = pl.BlockSpec((1, R, B), lambda i: (i, 0, 0))
    return pl.pallas_call(
        z_mid_kernel,
        out_shape=[shape(2, 3, R, B)] * 2,
        grid=(3,),
        in_specs=[first_half, one, second_half, one],
        out_specs=[first_half, second_half],
        input_output_aliases={0: 0, 2: 1},
        compiler_params=params(),
        cost_estimate=cost(2 * 3 * R * B, 6 * 3 * R * B * 2),
        name="z_mid",
    )(mid1, ra, mid3, rb)


def z_far_kernel(a, b, c, out):
    out[0] = (a[0, 0].astype(F32) + b[0, 0].astype(F32) + c[0, 0].astype(F32)).astype(BF)


def z_far(own, u, v):
    half = pl.BlockSpec((1, 1, R, B), lambda i: (1, i, 0, 0))
    return pl.pallas_call(
        z_far_kernel,
        out_shape=shape(3, R, B),
        grid=(3,),
        in_specs=[half] * 3,
        out_specs=pl.BlockSpec((1, R, B), lambda i: (i, 0, 0)),
        compiler_params=params(),
        cost_estimate=cost(2 * 3 * R * B, 4 * 3 * R * B * 2),
        name="z_far",
    )(own, u, v)


def swiglu_kernel(*refs):
    ins, (gu, hid) = refs[:-2], refs[-2:]

    def total(i):
        acc = None
        for ref in ins:
            term = (ref[0, i] if len(ref.shape) == 4 else ref[i]).astype(F32)
            acc = term if acc is None else acc + term
        return acc

    gate, up, grad = total(0), total(1), total(2)
    sig = jax.nn.sigmoid(gate)
    silu = gate * sig
    hid[...] = (silu * up).astype(BF)
    gu[0] = (grad * up * sig * (1.0 + gate * (1.0 - sig))).astype(BF)
    gu[1] = (grad * silu).astype(BF)


def swiglu(terms):
    specs = [
        pl.BlockSpec((1, 3, R, B), lambda i: (0, 0, 0, 0))
        if t.ndim == 4
        else pl.BlockSpec((3, R, B), lambda i: (0, 0, 0))
        for t in terms
    ]
    return pl.pallas_call(
        swiglu_kernel,
        out_shape=[shape(2, R, B), shape(R, B)],
        grid=(1,),
        in_specs=specs,
        out_specs=[
            pl.BlockSpec((2, R, B), lambda i: (0, 0, 0)),
            pl.BlockSpec((R, B), lambda i: (0, 0)),
        ],
        compiler_params=params(),
        cost_estimate=cost(40 * R * B, (len(terms) + 1) * 3 * R * B * 2),
        name="swiglu",
    )(*terms)


def scatter_x(send, keep):
    recv = narrow_move(send, 1, 0)
    s1, s2, s3 = x_sum(keep, recv)
    terms = [narrow_move(s1, 0, 1), narrow_move(s3, 0, 3), narrow_move(s2, 0, 2)]
    return [keep, recv, *terms]


def scatter_z(own, mid1, mid3, a2, b2):
    ra = narrow_move(a2, 0, 1)
    rb = narrow_move(b2, 0, 3)
    mid1, mid3 = z_mid(mid1, ra, mid3, rb)
    u = narrow_move(mid1, 0, 1)
    v = narrow_move(mid3, 0, 3)
    far = narrow_move(z_far(own, u, v), 1, 0)
    return [own, u, v, far]


def gather_x(block):
    before = narrow_move(block, 0, 1)
    after = narrow_move(block, 0, 3)
    across = narrow_move(block, 0, 2)
    far = narrow_move(jnp.stack([block, after, across, before]), 1, 0)
    near = [(block, None, 0, 0), (after, None, 0, 1), (across, None, 0, 2), (before, None, 0, 3)]
    return near + [(far, k, 1, k) for k in range(4)]


def gather_z(block):
    pair = jnp.stack([block, narrow_move(block, 1, 0)])
    before = narrow_move(pair, 0, 1)
    after = narrow_move(pair, 0, 3)
    near = narrow_move(before[0], 0, 1)
    far = narrow_move(after[1], 0, 3)
    blocks = [(near, None, 0, 2), (far, None, 1, 2)]
    for dz, source in ((0, pair), (1, after), (3, before)):
        blocks += [(source, k, k, dz) for k in range(2)]
    return blocks


def distinct(blocks):
    arrays, places = [], []
    for array, lead, dxh, dz in blocks:
        for n, seen in enumerate(arrays):
            if seen is array:
                break
        else:
            n = len(arrays)
            arrays.append(array)
        places.append((n, lead, dxh, dz))
    return arrays, places


def place(at, refs, places, i, target, rows):
    for n, lead, dxh, dz in places:
        value = refs[n][i] if lead is None else refs[n][lead, i]
        if rows is not None:
            value = jnp.where(rows, value, jnp.zeros_like(value))
        column = (lax.rem(at[0] + dxh, 2) * 4 + lax.rem(at[1] + dz, 4)) * B
        target[:, pl.ds(pl.multiple_of(column, B), B)] = value


def valid_rows(q, width):
    valid = FF - q * R
    if valid >= R:
        return None
    return lax.broadcasted_iota(jnp.int32, (R, width), 0) < valid


def whole(array):
    rank = array.ndim
    return pl.BlockSpec(array.shape, lambda *_: (0,) * rank)


def last_kernel(q, places, n_arrays, has_prev, is_end, at, *refs):
    refs = list(refs)
    arrays = [refs.pop(0) for _ in range(n_arrays)]
    xo, xt, wg, wu = [refs.pop(0) for _ in range(4)]
    if has_prev:
        acc_o, acc_t = refs.pop(0), refs.pop(0)
        refs.pop(0), refs.pop(0)
    gg, gu, out_o, out_t, ag, au = refs

    @pl.when(pl.program_id(0) == 0)
    def _():
        rows = valid_rows(q, B)
        place(at, arrays, places, 0, ag, rows)
        place(at, arrays, places, 1, au, rows)

    for out, act in ((gg, ag), (gu, au)):
        out[...] = (dot(act[:, :HALF], xo[0], NN) + dot(act[:, HALF:], xt[0], NN)).astype(BF)
    rows = valid_rows(q, N_BLOCK)
    vg, vu = wg[...], wu[...]
    if rows is not None:
        vg = jnp.where(rows, vg, jnp.zeros_like(vg))
        vu = jnp.where(rows, vu, jnp.zeros_like(vu))
    for k, out in enumerate((out_o, out_t)):
        part = slice(k * HALF, (k + 1) * HALF)
        total = dot(ag[:, part], vg, TN) + dot(au[:, part], vu, TN)
        if has_prev:
            total = total + (acc_o, acc_t)[k][...]
        out[...] = total.astype(out.dtype)


def last(q, is_end, at, blocks, xg_o, xg_t, wg, wu, prev):
    arrays, places = distinct(blocks)
    tokens = pl.BlockSpec((1, HALF, N_BLOCK), lambda n, at: (0, 0, n))
    weight = pl.BlockSpec((R, N_BLOCK), lambda n, at: (q, n))
    acc = pl.BlockSpec((HALF, N_BLOCK), lambda n, at: (0, n))
    operands = [*arrays, xg_o, xg_t, wg, wu]
    in_specs = [whole(a) for a in arrays] + [tokens, tokens, weight, weight]
    aliases = {}
    if prev is not None:
        n = len(operands) + 1
        gg, gu, acc_o, acc_t = prev
        operands += [acc_o, acc_t, gg, gu]
        in_specs += [acc, acc, pl.BlockSpec(memory_space=pl.ANY), pl.BlockSpec(memory_space=pl.ANY)]
        aliases = {n + 2: 0, n + 3: 1}
    acc_shape = shape(HALF, D, dtype=BF if is_end else F32)
    return pl.pallas_call(
        functools.partial(last_kernel, q, places, len(arrays), prev is not None, is_end),
        out_shape=[shape(FF, D), shape(FF, D), acc_shape, acc_shape],
        grid_spec=pltpu.PrefetchScalarGridSpec(
            num_scalar_prefetch=1,
            grid=(D // N_BLOCK,),
            in_specs=in_specs,
            out_specs=[weight, weight, acc, acc],
            scratch_shapes=[pltpu.VMEM((R, T), BF)] * 2,
        ),
        input_output_aliases=aliases,
        compiler_params=params(),
        cost_estimate=cost(4 * 2 * R * T * D, 2 * R * T * 2 + 4 * R * D * 2 + T * D * 10),
        name=f"last{q}",
    )(at, *operands)


def down_kernel(quarters, places, n_arrays, has_prev, at, *refs):
    refs = list(refs)
    arrays = [refs.pop(0) for _ in range(n_arrays)]
    go, gt = refs.pop(0), refs.pop(0)
    if has_prev:
        refs.pop(0)
    out, act = refs
    for i in range(len(quarters)):

        @pl.when((pl.program_id(0) == i) & (pl.program_id(1) == 0))
        def _(i=i):
            place(at, arrays, places, i, act, None)

    out[...] = (dot(act[:, :HALF], go[0], NN) + dot(act[:, HALF:], gt[0], NN)).astype(BF)


def down(quarters, at, blocks, xg_o, xg_t, prev):
    arrays, places = distinct(blocks)
    tokens = pl.BlockSpec((1, HALF, N_BLOCK), lambda i, n, at: (1, 0, n))
    stride = quarters[1] - quarters[0]
    out = pl.BlockSpec((R, N_BLOCK), lambda i, n, at: (quarters[0] + stride * i, n))
    operands = [*arrays, xg_o, xg_t]
    in_specs = [whole(a) for a in arrays] + [tokens, tokens]
    aliases = {}
    if prev is not None:
        aliases = {len(operands) + 1: 0}
        operands.append(prev)
        in_specs.append(pl.BlockSpec(memory_space=pl.ANY))
    return pl.pallas_call(
        functools.partial(down_kernel, quarters, places, len(arrays), prev is not None),
        out_shape=shape(FF, D),
        grid_spec=pltpu.PrefetchScalarGridSpec(
            num_scalar_prefetch=1,
            grid=(len(quarters), D // N_BLOCK),
            in_specs=in_specs,
            out_specs=out,
            scratch_shapes=[pltpu.VMEM((R, T), BF)],
        ),
        input_output_aliases=aliases,
        compiler_params=params(),
        cost_estimate=cost(len(quarters) * 2 * R * T * D, len(quarters) * 4 * R * T + T * D * 4),
        name=f"down{quarters[0]}",
    )(at, *operands)


def gather_tokens(inputs, grad_out):
    mine = jnp.stack([inputs, grad_out])
    pair = jnp.concatenate([mine, wide_move(mine, 0, 1, 0)], 1)
    around = [wide_move(pair, -dy, 0, 0) for dy in (1, 2, 3)]
    xg_o = jnp.concatenate([pair, *around], 1)
    return xg_o, wide_move(xg_o, 0, 0, 1)


def scatter_tokens(keep, send):
    recv = wide_move(send, 0, 0, 1)
    total = keep.astype(F32) + recv.astype(F32)
    parts = [total[dy * B : (dy + 1) * B] for dy in range(4)]
    acc = parts[0]
    for dy in (1, 3, 2):
        acc = acc + wide_move(parts[dy].astype(BF), dy, 0, 0).astype(F32)
    far = wide_move(acc[B // 2 :].astype(BF), 0, 1, 0)
    return (acc[: B // 2] + far.astype(F32)).astype(BF)


def body(inputs, grad_out, w_gate, w_up, w_down):
    narrow = lax.axis_index("narrow")
    at = jnp.stack([narrow // 4, narrow % 4]).astype(jnp.int32)
    xg_o, xg_t = gather_tokens(inputs, grad_out)
    wg, wu, wd = w_gate.T, w_up.T, w_down
    gu, hid = [], []
    for q in range(Q):
        is_x = q % 2 == 0
        products = first(q, is_x, at, xg_o, xg_t, wg, wu, wd)
        terms = scatter_x(*products) if is_x else scatter_z(*products)
        a, b = swiglu(terms)
        gu.append(a)
        hid.append(b)
    prev = None
    for q in range(Q):
        blocks = (gather_x if q % 2 == 0 else gather_z)(gu[q])
        prev = last(q, q == Q - 1, at, blocks, xg_o, xg_t, wg, wu, prev)
    grad_gate, grad_up, keep, send = prev
    grad_input = scatter_tokens(keep, send)
    grad_down = None
    for q in range(2):
        blocks = (gather_x if q == 0 else gather_z)(jnp.stack([hid[q], hid[q + 2]]))
        grad_down = down((q, q + 2), at, blocks, xg_o, xg_t, grad_down)
    return grad_input, grad_gate.T, grad_up.T, grad_down


def solution(mesh):
    return jax.shard_map(
        body,
        mesh=mesh,
        in_specs=(
            P("wide", "narrow"),
            P("wide", "narrow"),
            P("narrow", "wide"),
            P("narrow", "wide"),
            P("wide", "narrow"),
        ),
        out_specs=(
            P("wide", "narrow"),
            P("narrow", "wide"),
            P("narrow", "wide"),
            P("wide", "narrow"),
        ),
        check_vma=False,
    )
```

```python
import functools

import jax
import jax.numpy as jnp
from jax import lax
from jax.experimental import pallas as pl
from jax.experimental.pallas import tpu as pltpu
from jax.sharding import PartitionSpec as P

BF = jnp.bfloat16
F32 = jnp.float32
D = 1024
T = 1024
HALF = T // 2
B = 128
FF = 1848
RH = 928
R = RH // 2
N_BLOCK = 512
VMEM = 32 * 1024 * 1024
VMEM_FAR = 44 * 1024 * 1024
VMEM_SUMS = 12 * 1024 * 1024

NT = (((1,), (1,)), ((), ()))
NN = (((1,), (0,)), ((), ()))
TN = (((0,), (0,)), ((), ()))


def dot(a, b, dims):
    return lax.dot_general(a, b, dims, preferred_element_type=F32)


def shape(*dims, dtype=BF):
    return jax.ShapeDtypeStruct(dims, dtype)


def params(limit=VMEM):
    return pltpu.CompilerParams(vmem_limit_bytes=limit)


def cost(flops, nbytes):
    return pl.CostEstimate(flops=int(flops), bytes_accessed=int(nbytes), transcendentals=0)


def narrow_move(value, dxh, dz):
    pairs = [
        (xh * 4 + z, ((xh + dxh) % 2) * 4 + (z + dz) % 4) for xh in range(2) for z in range(4)
    ]
    return lax.ppermute(value, "narrow", pairs)


def wide_move(value, dy, dxl, dc):
    pairs = [
        (y * 4 + xl * 2 + c, ((y + dy) % 4) * 4 + ((xl + dxl) % 2) * 2 + (c + dc) % 2)
        for y in range(4)
        for xl in range(2)
        for c in range(2)
    ]
    return lax.ppermute(value, "wide", pairs)


def first_kernel(which, slots, layout, n_outs, at, *refs):
    sources = sorted({w // 2 for w in which})
    own, other, *refs = refs
    weights, refs = refs[: len(which)], refs[len(which) :]
    outs, refs = refs[:n_outs], refs[n_outs:]
    *targets, sems = refs

    @pl.when(pl.program_id(0) == 0)
    def _():
        copies = []
        for s, (dxh, dz) in enumerate(slots):
            row = pl.ds(pl.multiple_of(lax.rem(at[1] + dz, 4) * B, B), B)
            for k, (source, target) in enumerate(zip(sources, targets)):
                place_, sem = target.at[s * B : (s + 1) * B, :], sems.at[k, s]
                near = pltpu.make_async_copy(own.at[source, row, :], place_, sem)
                far = pltpu.make_async_copy(other.at[source, row, :], place_, sem)
                pl.when(at[0] == dxh)(near.start)
                pl.when(at[0] != dxh)(far.start)
                copies.append(near)
        for copy in copies:
            copy.wait()

    for i, w in enumerate(which):
        res = dot(weights[i][...], targets[sources.index(w // 2)][...], NT).astype(BF)

        def store(outs):
            for out, members in zip(outs, layout):
                for k, s in enumerate(members):
                    value = res[:, s * B : (s + 1) * B]
                    if len(members) > 1:
                        out[k, i] = value
                    else:
                        out[i] = value

        if len(outs) == len(layout):
            store(outs)
        else:
            pl.when(pl.program_id(0) < 2)(functools.partial(store, outs[: len(layout)]))
            pl.when(pl.program_id(0) >= 2)(functools.partial(store, outs[len(layout) :]))


def rows_spec(array, lead=None, step=lambda r: r):
    if array.ndim == 3:
        return pl.BlockSpec((array.shape[0], R, B), lambda r, *_: (0, step(r), 0))
    if lead is None:
        return pl.BlockSpec((*array.shape[:2], R, B), lambda r, *_: (0, 0, step(r), 0))
    return pl.BlockSpec((1, array.shape[1], R, B), lambda r, *_: (lead, 0, step(r), 0))


def first(name, half, slots, layout, at, halves, weights):
    which = (0, 1, 2)
    n = len(which)
    base = 0 if half is None else 2 * half
    weight = pl.BlockSpec((R, D), lambda r, at: (base + r, 0))
    out_shape = [shape(len(m), n, RH, B) if len(m) > 1 else shape(n, RH, B) for m in layout]
    out_specs = [rows_spec(o) for o in out_shape]
    if half is None:
        out_specs = [rows_spec(o, step=lambda r: jnp.minimum(r, 1)) for o in out_shape]
        out_specs += [rows_spec(o, step=lambda r: jnp.maximum(r - 2, 0)) for o in out_shape]
        out_shape = out_shape * 2
    width = len(slots) * B
    steps = 4 if half is None else 2
    return pl.pallas_call(
        functools.partial(first_kernel, which, slots, layout, len(out_shape)),
        out_shape=out_shape,
        grid_spec=pltpu.PrefetchScalarGridSpec(
            num_scalar_prefetch=1,
            grid=(steps,),
            in_specs=[pl.BlockSpec(memory_space=pl.ANY)] * 2 + [weight] * n,
            out_specs=out_specs,
            scratch_shapes=[
                *[pltpu.VMEM((width, D), BF)] * 2,
                pltpu.SemaphoreType.DMA((2, len(slots))),
            ],
        ),
        compiler_params=params(VMEM_FAR if half is None else VMEM),
        cost_estimate=cost(n * 2 * steps * R * width * D, n * steps * R * (D + width) * 2),
        name=name,
    )(at, *halves, *[weights[w] for w in which])


def pick(group, lead, i):
    for ref in group:
        rank = len(ref.shape)
        n = ref.shape[rank - 3]
        if i < n:
            return (ref[lead, i] if rank == 4 else ref[i]).astype(F32)
        i -= n


def grouped(refs, sizes):
    refs = list(refs)
    return [[refs.pop(0) for _ in range(size)] for size in sizes]


def on_groups(name, kernel, groups, out_shape, leads=None):
    leads = leads or [None] * len(groups)
    sizes = [len(g) for g in groups]
    n = sum(sizes)
    arrays = [a for g in groups for a in g]

    def run(*refs):
        kernel(grouped(refs[:n], sizes), refs[n:])

    moved = sum(a.size for a in arrays) + sum(o.size for o in out_shape)
    return pl.pallas_call(
        run,
        out_shape=out_shape,
        grid=(2,),
        in_specs=[rows_spec(a, lead) for g, lead in zip(groups, leads) for a in g],
        out_specs=[rows_spec(o) for o in out_shape],
        compiler_params=params(VMEM_SUMS),
        cost_estimate=cost(moved, moved * 2),
        name=name,
    )(*arrays)


def x_sum(keep, recv, first_lead):
    one = recv.ndim == 3
    n = 1 if one else recv.shape[0]

    def kernel(groups, outs):
        for k, out in enumerate(outs):
            for i in range(3):
                out[i] = (pick(groups[0], first_lead + k, i) + pick(groups[1], k, i)).astype(BF)

    return on_groups(f"x_sum{n}", kernel, [(keep,), (recv,)], [shape(3, RH, B)] * n)


def z_mid(mid1, ra, mid3, rb):
    def kernel(groups, outs):
        for i in range(3):
            outs[0][0, i] = (pick(groups[0], 0, i) + pick(groups[1], 0, i)).astype(BF)
            outs[0][1, i] = pick(groups[0], 1, i).astype(BF)
            outs[1][0, i] = pick(groups[2], 0, i).astype(BF)
            outs[1][1, i] = (pick(groups[2], 1, i) + pick(groups[3], 1, i)).astype(BF)

    return on_groups("z_mid", kernel, [mid1, ra, mid3, rb], [shape(2, 3, RH, B)] * 2)


def z_far(own, u, v):
    def kernel(groups, outs):
        for i in range(3):
            total = pick(groups[0], 0, i) + pick(groups[1], 0, i) + pick(groups[2], 0, i)
            outs[0][i] = total.astype(BF)

    groups = [(own,), (u,), (v,)]
    return on_groups("z_far", kernel, groups, [shape(3, RH, B)], leads=[1, 1, 1])[0]


def swiglu(x_terms, z_terms):
    terms = [*x_terms, *z_terms]

    def kernel(groups, outs):
        alone, both = outs
        for k, mine in enumerate((groups[: len(x_terms)], groups[len(x_terms) :])):
            sums = []
            for i in range(3):
                acc = pick(mine[0], 0, i)
                for group in mine[1:]:
                    acc = acc + pick(group, 0, i)
                sums.append(acc)
            gate, up, grad = sums
            sig = jax.nn.sigmoid(gate)
            silu = gate * sig
            gate_grad = grad * up * sig * (1.0 + gate * (1.0 - sig))
            for i, value in enumerate((gate_grad, grad * silu, silu * up)):
                value = value.astype(BF)
                both[k, i] = value
                if k == 0:
                    alone[i] = value

    out_shape = [shape(3, RH, B), shape(2, 3, RH, B)]
    groups, leads = [(t,) for t, _ in terms], [lead for _, lead in terms]
    return on_groups("swiglu", kernel, groups, out_shape, leads=leads)


def distinct(blocks):
    arrays, places = [], []
    for array, lead, base, dxh, dz in blocks:
        for n, seen in enumerate(arrays):
            if seen is array:
                break
        else:
            n = len(arrays)
            arrays.append(array)
        places.append((n, lead, base, dxh, dz))
    return arrays, places


def place_copies(at, refs, places, targets, sems):
    copies = []
    for k, (n, lead, base, dxh, dz) in enumerate(places):
        column = (lax.rem(at[0] + dxh, 2) * 4 + lax.rem(at[1] + dz, 4)) * B
        part = pl.ds(pl.multiple_of(column, B), B)
        for i, target in enumerate(targets):
            source = refs[n].at[base + i] if lead is None else refs[n].at[lead, base + i]
            copies.append(pltpu.make_async_copy(source, target.at[:, part], sems.at[i, k]))
    return copies


def back_kernel(places, counts, at, *refs):
    refs = list(refs)
    arrays = [[refs.pop(0) for _ in range(count)] for count in counts]
    wg, wu, out_o, out_t, *acts, sems = refs
    halves = (slice(0, RH), slice(RH, 2 * RH))

    @pl.when(pl.program_id(0) == 0)
    def _():
        copies = []
        for half in range(2):
            targets = [act.at[halves[half], :] for act in acts]
            copies += place_copies(at, arrays[half], places[half], targets, sems.at[half])
        for copy in copies:
            copy.start()
        for copy in copies:
            copy.wait()
        last = slice(2 * RH - 16, 2 * RH)
        rows = lax.broadcasted_iota(jnp.int32, (16, T), 0) < FF - (2 * RH - 16)
        for act in acts:
            act[last, :] = jnp.where(rows, act[last, :], jnp.zeros((16, T), BF))

    rows = lax.broadcasted_iota(jnp.int32, (2 * RH, N_BLOCK), 0) < FF
    vg = jnp.where(rows, wg[...], jnp.zeros((2 * RH, N_BLOCK), BF))
    vu = jnp.where(rows, wu[...], jnp.zeros((2 * RH, N_BLOCK), BF))
    for k, out in enumerate((out_o, out_t)):
        part = slice(k * HALF, (k + 1) * HALF)
        total = dot(acts[0][:, part], vg, TN) + dot(acts[1][:, part], vu, TN)
        out[...] = total.astype(out.dtype)


def back(at, blocks_x, blocks_z, weights):
    (arrays_x, places_x), (arrays_z, places_z) = distinct(blocks_x), distinct(blocks_z)
    arrays = arrays_x + arrays_z
    weight = pl.BlockSpec((2 * RH, N_BLOCK), lambda n, at: (0, n))
    out = pl.BlockSpec((HALF, N_BLOCK), lambda n, at: (0, n))
    counts = (len(arrays_x), len(arrays_z))
    return pl.pallas_call(
        functools.partial(back_kernel, (places_x, places_z), counts),
        out_shape=[shape(HALF, D)] * 2,
        grid_spec=pltpu.PrefetchScalarGridSpec(
            num_scalar_prefetch=1,
            grid=(D // N_BLOCK,),
            in_specs=[pl.BlockSpec(memory_space=pl.ANY)] * len(arrays) + [weight] * 2,
            out_specs=[out] * 2,
            scratch_shapes=[pltpu.VMEM((2 * RH, T), BF)] * 2 + [pltpu.SemaphoreType.DMA((2, 2, 8))],
        ),
        compiler_params=params(),
        cost_estimate=cost(2 * 2 * FF * T * D, 2 * FF * (T + D) * 2 + T * D * 2),
        name="back",
    )(at, *arrays, *weights[:2])


def grads_kernel(places, counts, n, at, *refs):
    refs = list(refs)
    arrays = [[refs.pop(0) for _ in range(count)] for count in counts]
    own, other, *refs = refs
    outs, acts, tokens, sems = refs[:n], refs[n : 2 * n], refs[2 * n], refs[2 * n + 1]
    halves = (slice(0, RH), slice(RH, 2 * RH))
    copies = []
    for half in range(2):
        targets = [act.at[halves[half], :] for act in acts]
        copies.append(place_copies(at, arrays[half], places[half], targets, sems.at[half]))
    start = pl.program_id(0) == 0

    @pl.when(start)
    def _():
        for copy in copies[0] + copies[1]:
            copy.start()

    tokens[:HALF, :] = own[0]
    tokens[HALF:, :] = other[0]
    for half, rows in enumerate(halves):

        @pl.when(start)
        def _(half=half):
            for copy in copies[half]:
                copy.wait()

        for out, act in zip(outs, acts):
            out[rows, :] = dot(act[rows, :], tokens[...], NN).astype(BF)


def grads(name, n, at, blocks_x, blocks_z, k, halves):
    (arrays_x, places_x), (arrays_z, places_z) = distinct(blocks_x), distinct(blocks_z)
    arrays = arrays_x + arrays_z
    token = pl.BlockSpec((1, HALF, N_BLOCK), lambda n, at: (k, 0, n))
    out = pl.BlockSpec((2 * RH, N_BLOCK), lambda n, at: (0, n))
    counts = (len(arrays_x), len(arrays_z))
    return pl.pallas_call(
        functools.partial(grads_kernel, (places_x, places_z), counts, n),
        out_shape=[shape(FF, D)] * n,
        grid_spec=pltpu.PrefetchScalarGridSpec(
            num_scalar_prefetch=1,
            grid=(D // N_BLOCK,),
            in_specs=[pl.BlockSpec(memory_space=pl.ANY)] * len(arrays) + [token] * 2,
            out_specs=[out] * n,
            scratch_shapes=[
                *[pltpu.VMEM((2 * RH, T), BF)] * n,
                pltpu.VMEM((T, N_BLOCK), BF),
                pltpu.SemaphoreType.DMA((2, n, 8)),
            ],
        ),
        compiler_params=params(),
        cost_estimate=cost(n * 2 * FF * T * D, n * FF * (T + D) * 2 + T * D * 2),
        name=name,
    )(at, *arrays, *halves)


def after(value, *earlier):
    return lax.optimization_barrier((value, *earlier))[0]


def scatter_tokens(keep, recv):
    total = keep.astype(F32) + recv.astype(F32)
    parts = [total[dy * B : (dy + 1) * B] for dy in range(4)]
    acc = parts[0]
    for dy in (1, 3, 2):
        acc = acc + wide_move(parts[dy].astype(BF), dy, 0, 0).astype(F32)
    far = wide_move(acc[B // 2 :].astype(BF), 0, 1, 0)
    return (acc[: B // 2] + far.astype(F32)).astype(BF)


def body(inputs, grad_out, w_gate, w_up, w_down):
    narrow = lax.axis_index("narrow")
    at = jnp.stack([narrow // 4, narrow % 4]).astype(jnp.int32)
    weights = (w_gate.T, w_up.T, w_down)
    wg, wu = weights[:2]

    pair = jnp.concatenate([inputs, wide_move(inputs, 0, 1, 0)])
    grads_y = jnp.stack([grad_out, *[wide_move(grad_out, -dy, 0, 0) for dy in (1, 2, 3)]])
    pairs = [pair, *[wide_move(pair, -dy, 0, 0) for dy in (1, 2, 3)]]
    grads_x = wide_move(grads_y, 0, 1, 0)
    pairs_g = jnp.stack([grads_y, grads_x], 1).reshape(HALF, D)
    tokens = jnp.stack([jnp.concatenate(pairs), pairs_g])
    halves = (tokens, wide_move(tokens, 0, 0, 1))

    keep2, send2, a2, b2 = first("far", None, ((0, 2), (1, 2)), ((0,), (1,)), at, halves, weights)
    recv2 = narrow_move(send2, 1, 0)
    ra, rb = narrow_move(a2, 0, 1), narrow_move(b2, 0, 3)
    (send,) = first("send", 0, ((1, 1), (1, 3)), ((0, 1),), after(at, a2), halves, weights)
    recv = narrow_move(send, 1, 0)
    mid_slots = ((0, 1), (1, 1), (0, 3), (1, 3))
    mid1, mid3 = first("mid", 1, mid_slots, ((0, 1), (2, 3)), after(at, send), halves, weights)
    u, v = z_mid((mid1,), (ra,), (mid3,), (rb,))
    u, v = after(u, recv2), after(v, recv2)
    u, v = narrow_move(u, 0, 1), narrow_move(v, 0, 3)
    (s2,) = x_sum(keep2, recv2, 0)
    s2 = narrow_move(s2, 0, 2)
    keep_slots = ((1, 0), (0, 0), (0, 1), (0, 3))
    send_0, keep = first("keep", 0, keep_slots, ((0,), (1, 2, 3)), after(at, mid1), halves, weights)
    recv_0 = narrow_move(send_0, 1, 0)
    (own,) = first("own", 1, ((0, 0), (1, 0)), ((0, 1),), after(at, keep), halves, weights)
    far = narrow_move(z_far(own, u, v), 1, 0)
    s1, s3 = x_sum(keep, recv, 1)
    s1, s3 = narrow_move(s1, 0, 1), narrow_move(s3, 0, 3)
    alone, both = swiglu(
        [(keep, 0), (recv_0, None), (s1, None), (s2, None), (s3, None)],
        [(own, 0), (u, 0), (v, 0), (far, None)],
    )

    before, after_, across = [narrow_move(alone, 0, dz) for dz in (1, 3, 2)]
    swapped = narrow_move(both, 1, 0)
    ready = (before, after_, across, swapped)

    def far_blocks(part):
        return after(jnp.stack([t[part] for t in (after_, across, before)]), *ready)

    def pair_of(part):
        return after(jnp.stack([both[1, part], swapped[1, part]]), *ready)

    def x_blocks(first, rest):
        near = [(alone, None, 0, 0), (after_, None, 0, 1), (across, None, 0, 2), (before, None, 0, 3)]
        far = [(swapped, 0, 1, 0)] + [(rest, k, 1, k + 1) for k in range(3)]
        return [(a, lead, first if a is not rest else 0, *at_) for a, lead, *at_ in near + far]

    def z_blocks(first, pair, after_, before, near, far):
        blocks = [(near, None, 0, 0, 2), (far, None, 0, 1, 2)]
        for dz, source in ((0, pair), (1, after_), (3, before)):
            blocks += [(source, k, 0, k, dz) for k in range(2)]
        return blocks

    gu, hid = slice(0, 2), slice(2, 3)
    pair = pair_of(gu)
    z_before, z_after = narrow_move(pair, 0, 1), narrow_move(pair, 0, 3)
    rest = narrow_move(far_blocks(gu), 1, 0)
    near, far = narrow_move(z_before[0], 0, 1), narrow_move(z_after[1], 0, 3)
    blocks_x = x_blocks(0, rest)
    blocks_z = z_blocks(0, pair, z_after, z_before, near, far)

    pair = after(pair_of(hid), z_before, z_after)
    z_before, z_after = narrow_move(pair, 0, 1), narrow_move(pair, 0, 3)
    rest_hid = narrow_move(after(far_blocks(hid), rest), 1, 0)
    hid_near, hid_far = narrow_move(z_before[0], 0, 1), narrow_move(z_after[1], 0, 3)
    hid_x = x_blocks(2, rest_hid)
    hid_z = z_blocks(2, pair, z_after, z_before, hid_near, hid_far)

    keep, send = back(after(at, z_before, z_after), blocks_x, blocks_z, weights)
    from_core = wide_move(send, 0, 0, 1)
    grad_input = scatter_tokens(keep, from_core)

    grad_gate, grad_up = grads("grads", 2, after(at, from_core, hid_near, hid_far), blocks_x, blocks_z, 0, halves)
    (grad_down,) = grads("down", 1, after(at, grad_gate), hid_x, hid_z, 1, halves)
    return grad_input, grad_gate.T, grad_up.T, grad_down


def solution(mesh):
    return jax.shard_map(
        body,
        mesh=mesh,
        in_specs=(
            P("wide", "narrow"),
            P("wide", "narrow"),
            P("narrow", "wide"),
            P("narrow", "wide"),
            P("wide", "narrow"),
        ),
        out_specs=(
            P("wide", "narrow"),
            P("narrow", "wide"),
            P("narrow", "wide"),
            P("wide", "narrow"),
        ),
        check_vma=False,
    )
```

```python
import functools

import jax
import jax.numpy as jnp
from jax import lax
from jax.experimental import pallas as pl
from jax.experimental.pallas import tpu as pltpu
from jax.sharding import PartitionSpec as P

BF = jnp.bfloat16
F32 = jnp.float32
D = 1024
T = 1024
HALF = T // 2
B = 128
FF = 1848
RH = 928
R = RH // 2
N_BLOCK = 512
VMEM = 32 * 1024 * 1024
VMEM_FAR = 48 * 1024 * 1024
VMEM_SUMS = 12 * 1024 * 1024

NT = (((1,), (1,)), ((), ()))
NN = (((1,), (0,)), ((), ()))
TN = (((0,), (0,)), ((), ()))


def dot(a, b, dims):
    return lax.dot_general(a, b, dims, preferred_element_type=F32)


def shape(*dims, dtype=BF):
    return jax.ShapeDtypeStruct(dims, dtype)


def params(limit=VMEM):
    return pltpu.CompilerParams(vmem_limit_bytes=limit)


def cost(flops, nbytes):
    return pl.CostEstimate(flops=int(flops), bytes_accessed=int(nbytes), transcendentals=0)


def narrow_move(value, dxh, dz):
    pairs = [
        (xh * 4 + z, ((xh + dxh) % 2) * 4 + (z + dz) % 4) for xh in range(2) for z in range(4)
    ]
    return lax.ppermute(value, "narrow", pairs)


def wide_move(value, dy, dxl, dc):
    pairs = [
        (y * 4 + xl * 2 + c, ((y + dy) % 4) * 4 + ((xl + dxl) % 2) * 2 + (c + dc) % 2)
        for y in range(4)
        for xl in range(2)
        for c in range(2)
    ]
    return lax.ppermute(value, "wide", pairs)


def first_kernel(which, slots, layout, n_outs, at, *refs):
    sources = sorted({w // 2 for w in which})
    own, other, *refs = refs
    weights, refs = refs[: len(which)], refs[len(which) :]
    outs, refs = refs[:n_outs], refs[n_outs:]
    *targets, sems = refs

    @pl.when(pl.program_id(0) == 0)
    def _():
        copies = []
        for s, (dxh, dz) in enumerate(slots):
            row = pl.ds(pl.multiple_of(lax.rem(at[1] + dz, 4) * B, B), B)
            for k, (source, target) in enumerate(zip(sources, targets)):
                place_, sem = target.at[s * B : (s + 1) * B, :], sems.at[k, s]
                near = pltpu.make_async_copy(own.at[source, row, :], place_, sem)
                far = pltpu.make_async_copy(other.at[source, row, :], place_, sem)
                pl.when(at[0] == dxh)(near.start)
                pl.when(at[0] != dxh)(far.start)
                copies.append(near)
        for copy in copies:
            copy.wait()

    for i, w in enumerate(which):
        res = dot(weights[i][...], targets[sources.index(w // 2)][...], NT).astype(BF)
        for out, members in zip(outs, layout):
            for k, s in enumerate(members):
                value = res[:, s * B : (s + 1) * B]
                if len(members) > 1:
                    out[k, i] = value
                else:
                    out[i] = value


def rows_spec(array, lead=None, step=lambda r: r):
    if array.ndim == 3:
        return pl.BlockSpec((array.shape[0], R, B), lambda r, *_: (0, step(r), 0))
    if lead is None:
        return pl.BlockSpec((*array.shape[:2], R, B), lambda r, *_: (0, 0, step(r), 0))
    return pl.BlockSpec((1, array.shape[1], R, B), lambda r, *_: (lead, 0, step(r), 0))


def first(name, half, slots, layout, at, halves, weights, limit=VMEM):
    which = (0, 1, 2)
    n = len(which)
    weight = pl.BlockSpec((R, D), lambda r, at: (2 * half + r, 0))
    out_shape = [shape(len(m), n, RH, B) if len(m) > 1 else shape(n, RH, B) for m in layout]
    out_specs = [rows_spec(o) for o in out_shape]
    width = len(slots) * B
    steps = 2
    return pl.pallas_call(
        functools.partial(first_kernel, which, slots, layout, len(out_shape)),
        out_shape=out_shape,
        grid_spec=pltpu.PrefetchScalarGridSpec(
            num_scalar_prefetch=1,
            grid=(steps,),
            in_specs=[pl.BlockSpec(memory_space=pl.ANY)] * 2 + [weight] * n,
            out_specs=out_specs,
            scratch_shapes=[
                *[pltpu.VMEM((width, D), BF)] * 2,
                pltpu.SemaphoreType.DMA((2, len(slots))),
            ],
        ),
        compiler_params=params(limit),
        cost_estimate=cost(n * 2 * steps * R * width * D, n * steps * R * (D + width) * 2),
        name=name,
    )(at, *halves, *[weights[w] for w in which])


def pick(group, lead, i):
    for ref in group:
        rank = len(ref.shape)
        n = ref.shape[rank - 3]
        if i < n:
            return (ref[lead, i] if rank == 4 else ref[i]).astype(F32)
        i -= n


def grouped(refs, sizes):
    refs = list(refs)
    return [[refs.pop(0) for _ in range(size)] for size in sizes]


def on_groups(name, kernel, groups, out_shape, leads=None):
    leads = leads or [None] * len(groups)
    sizes = [len(g) for g in groups]
    n = sum(sizes)
    arrays = [a for g in groups for a in g]

    def run(*refs):
        kernel(grouped(refs[:n], sizes), refs[n:])

    moved = sum(a.size for a in arrays) + sum(o.size for o in out_shape)
    return pl.pallas_call(
        run,
        out_shape=out_shape,
        grid=(2,),
        in_specs=[rows_spec(a, lead) for g, lead in zip(groups, leads) for a in g],
        out_specs=[rows_spec(o) for o in out_shape],
        compiler_params=params(VMEM_SUMS),
        cost_estimate=cost(moved, moved * 2),
        name=name,
    )(*arrays)


def x_sum(keep, recv, first_lead):
    one = recv.ndim == 3
    n = 1 if one else recv.shape[0]

    def kernel(groups, outs):
        for k, out in enumerate(outs):
            for i in range(3):
                out[i] = (pick(groups[0], first_lead + k, i) + pick(groups[1], k, i)).astype(BF)

    return on_groups(f"x_sum{n}", kernel, [(keep,), (recv,)], [shape(3, RH, B)] * n)


def z_mid(mid1, ra, mid3, rb):
    def kernel(groups, outs):
        for i in range(3):
            outs[0][0, i] = (pick(groups[0], 0, i) + pick(groups[1], 0, i)).astype(BF)
            outs[0][1, i] = pick(groups[0], 1, i).astype(BF)
            outs[1][0, i] = pick(groups[2], 0, i).astype(BF)
            outs[1][1, i] = (pick(groups[2], 1, i) + pick(groups[3], 1, i)).astype(BF)

    return on_groups("z_mid", kernel, [mid1, ra, mid3, rb], [shape(2, 3, RH, B)] * 2)


def z_far(own, u, v):
    def kernel(groups, outs):
        for i in range(3):
            total = pick(groups[0], 0, i) + pick(groups[1], 0, i) + pick(groups[2], 0, i)
            outs[0][i] = total.astype(BF)

    groups = [(own,), (u,), (v,)]
    return on_groups("z_far", kernel, groups, [shape(3, RH, B)], leads=[1, 1, 1])[0]


def swiglu(x_terms, z_terms):
    terms = [*x_terms, *z_terms]

    def kernel(groups, outs):
        alone, both = outs
        for k, mine in enumerate((groups[: len(x_terms)], groups[len(x_terms) :])):
            sums = []
            for i in range(3):
                acc = pick(mine[0], 0, i)
                for group in mine[1:]:
                    acc = acc + pick(group, 0, i)
                sums.append(acc)
            gate, up, grad = sums
            sig = jax.nn.sigmoid(gate)
            silu = gate * sig
            gate_grad = grad * up * sig * (1.0 + gate * (1.0 - sig))
            for i, value in enumerate((gate_grad, grad * silu, silu * up)):
                value = value.astype(BF)
                both[k, i] = value
                if k == 0:
                    alone[i] = value

    out_shape = [shape(3, RH, B), shape(2, 3, RH, B)]
    groups, leads = [(t,) for t, _ in terms], [lead for _, lead in terms]
    return on_groups("swiglu", kernel, groups, out_shape, leads=leads)


def distinct(blocks):
    arrays, places = [], []
    for array, lead, base, dxh, dz in blocks:
        for n, seen in enumerate(arrays):
            if seen is array:
                break
        else:
            n = len(arrays)
            arrays.append(array)
        places.append((n, lead, base, dxh, dz))
    return arrays, places


def place_copies(at, refs, places, targets, sems):
    copies = []
    for k, (n, lead, base, dxh, dz) in enumerate(places):
        column = (lax.rem(at[0] + dxh, 2) * 4 + lax.rem(at[1] + dz, 4)) * B
        part = pl.ds(pl.multiple_of(column, B), B)
        for i, target in enumerate(targets):
            source = refs[n].at[base + i] if lead is None else refs[n].at[lead, base + i]
            copies.append(pltpu.make_async_copy(source, target.at[:, part], sems.at[i, k]))
    return copies


def back_kernel(places, counts, at, *refs):
    refs = list(refs)
    arrays = [[refs.pop(0) for _ in range(count)] for count in counts]
    wg, wu, out_o, out_t, *acts, sems = refs
    halves = (slice(0, RH), slice(RH, 2 * RH))

    @pl.when(pl.program_id(0) == 0)
    def _():
        copies = []
        for half in range(2):
            targets = [act.at[halves[half], :] for act in acts]
            copies += place_copies(at, arrays[half], places[half], targets, sems.at[half])
        for copy in copies:
            copy.start()
        for copy in copies:
            copy.wait()
        last = slice(2 * RH - 16, 2 * RH)
        rows = lax.broadcasted_iota(jnp.int32, (16, T), 0) < FF - (2 * RH - 16)
        for act in acts:
            act[last, :] = jnp.where(rows, act[last, :], jnp.zeros((16, T), BF))

    rows = lax.broadcasted_iota(jnp.int32, (2 * RH, N_BLOCK), 0) < FF
    vg = jnp.where(rows, wg[...], jnp.zeros((2 * RH, N_BLOCK), BF))
    vu = jnp.where(rows, wu[...], jnp.zeros((2 * RH, N_BLOCK), BF))
    for k, out in enumerate((out_o, out_t)):
        part = slice(k * HALF, (k + 1) * HALF)
        total = dot(acts[0][:, part], vg, TN) + dot(acts[1][:, part], vu, TN)
        out[...] = total.astype(out.dtype)


def back(at, blocks_x, blocks_z, weights):
    (arrays_x, places_x), (arrays_z, places_z) = distinct(blocks_x), distinct(blocks_z)
    arrays = arrays_x + arrays_z
    weight = pl.BlockSpec((2 * RH, N_BLOCK), lambda n, at: (0, n))
    out = pl.BlockSpec((HALF, N_BLOCK), lambda n, at: (0, n))
    counts = (len(arrays_x), len(arrays_z))
    return pl.pallas_call(
        functools.partial(back_kernel, (places_x, places_z), counts),
        out_shape=[shape(HALF, D)] * 2,
        grid_spec=pltpu.PrefetchScalarGridSpec(
            num_scalar_prefetch=1,
            grid=(D // N_BLOCK,),
            in_specs=[pl.BlockSpec(memory_space=pl.ANY)] * len(arrays) + [weight] * 2,
            out_specs=[out] * 2,
            scratch_shapes=[pltpu.VMEM((2 * RH, T), BF)] * 2 + [pltpu.SemaphoreType.DMA((2, 2, 8))],
        ),
        compiler_params=params(),
        cost_estimate=cost(2 * 2 * FF * T * D, 2 * FF * (T + D) * 2 + T * D * 2),
        name="back",
    )(at, *arrays, *weights[:2])


def grads_kernel(places, counts, n, at, *refs):
    refs = list(refs)
    arrays = [[refs.pop(0) for _ in range(count)] for count in counts]
    own, other, *refs = refs
    outs, acts, tokens, sems = refs[:n], refs[n : 2 * n], refs[2 * n], refs[2 * n + 1]
    halves = (slice(0, RH), slice(RH, 2 * RH))
    copies = []
    for half in range(2):
        targets = [act.at[halves[half], :] for act in acts]
        copies.append(place_copies(at, arrays[half], places[half], targets, sems.at[half]))
    start = pl.program_id(0) == 0

    @pl.when(start)
    def _():
        for copy in copies[0] + copies[1]:
            copy.start()

    tokens[:HALF, :] = own[0]
    tokens[HALF:, :] = other[0]
    for half, rows in enumerate(halves):

        @pl.when(start)
        def _(half=half):
            for copy in copies[half]:
                copy.wait()

        for out, act in zip(outs, acts):
            out[rows, :] = dot(act[rows, :], tokens[...], NN).astype(BF)


def grads(name, n, at, blocks_x, blocks_z, k, halves):
    (arrays_x, places_x), (arrays_z, places_z) = distinct(blocks_x), distinct(blocks_z)
    arrays = arrays_x + arrays_z
    token = pl.BlockSpec((1, HALF, N_BLOCK), lambda n, at: (k, 0, n))
    out = pl.BlockSpec((2 * RH, N_BLOCK), lambda n, at: (0, n))
    counts = (len(arrays_x), len(arrays_z))
    return pl.pallas_call(
        functools.partial(grads_kernel, (places_x, places_z), counts, n),
        out_shape=[shape(FF, D)] * n,
        grid_spec=pltpu.PrefetchScalarGridSpec(
            num_scalar_prefetch=1,
            grid=(D // N_BLOCK,),
            in_specs=[pl.BlockSpec(memory_space=pl.ANY)] * len(arrays) + [token] * 2,
            out_specs=[out] * n,
            scratch_shapes=[
                *[pltpu.VMEM((2 * RH, T), BF)] * n,
                pltpu.VMEM((T, N_BLOCK), BF),
                pltpu.SemaphoreType.DMA((2, n, 8)),
            ],
        ),
        compiler_params=params(),
        cost_estimate=cost(n * 2 * FF * T * D, n * FF * (T + D) * 2 + T * D * 2),
        name=name,
    )(at, *arrays, *halves)


def after(value, *earlier):
    return lax.optimization_barrier((value, *earlier))[0]


def scatter_tokens(keep, recv):
    total = keep.astype(F32) + recv.astype(F32)
    parts = [total[dy * B : (dy + 1) * B] for dy in range(4)]
    acc = parts[0]
    for dy in (1, 3, 2):
        acc = acc + wide_move(parts[dy].astype(BF), dy, 0, 0).astype(F32)
    far = wide_move(acc[B // 2 :].astype(BF), 0, 1, 0)
    return (acc[: B // 2] + far.astype(F32)).astype(BF)


def body(inputs, grad_out, w_gate, w_up, w_down):
    narrow = lax.axis_index("narrow")
    at = jnp.stack([narrow // 4, narrow % 4]).astype(jnp.int32)
    weights = (w_gate.T, w_up.T, w_down)
    wg, wu = weights[:2]

    pair = jnp.concatenate([inputs, wide_move(inputs, 0, 1, 0)])
    grads_y = jnp.stack([grad_out, *[wide_move(grad_out, -dy, 0, 0) for dy in (1, 2, 3)]])
    pairs = [pair, *[wide_move(pair, -dy, 0, 0) for dy in (1, 2, 3)]]
    grads_x = wide_move(grads_y, 0, 1, 0)
    pairs_g = jnp.stack([grads_y, grads_x], 1).reshape(HALF, D)
    tokens = jnp.stack([jnp.concatenate(pairs), pairs_g])
    halves = (tokens, wide_move(tokens, 0, 0, 1))

    far_slots = ((0, 2), (1, 2))
    a2, b2 = first("ring", 1, far_slots, ((0,), (1,)), at, halves, weights, VMEM_FAR)
    keep2, send2 = first("far", 0, far_slots, ((0,), (1,)), after(at, a2), halves, weights, VMEM_FAR)
    recv2 = narrow_move(send2, 1, 0)
    ra, rb = narrow_move(a2, 0, 1), narrow_move(b2, 0, 3)
    (send,) = first("send", 0, ((1, 1), (1, 3)), ((0, 1),), after(at, keep2), halves, weights)
    recv = narrow_move(send, 1, 0)
    mid_slots = ((0, 1), (1, 1), (0, 3), (1, 3))
    mid1, mid3 = first("mid", 1, mid_slots, ((0, 1), (2, 3)), after(at, send), halves, weights)
    u, v = z_mid((mid1,), (ra,), (mid3,), (rb,))
    u, v = after(u, recv2), after(v, recv2)
    u, v = narrow_move(u, 0, 1), narrow_move(v, 0, 3)
    (s2,) = x_sum(keep2, recv2, 0)
    s2 = narrow_move(s2, 0, 2)
    keep_slots = ((1, 0), (0, 0), (0, 1), (0, 3))
    send_0, keep = first("keep", 0, keep_slots, ((0,), (1, 2, 3)), after(at, mid1), halves, weights)
    recv_0 = narrow_move(send_0, 1, 0)
    (own,) = first("own", 1, ((0, 0), (1, 0)), ((0, 1),), after(at, keep), halves, weights)
    far = narrow_move(z_far(own, u, v), 1, 0)
    s1, s3 = x_sum(keep, recv, 1)
    s1, s3 = narrow_move(s1, 0, 1), narrow_move(s3, 0, 3)
    alone, both = swiglu(
        [(keep, 0), (recv_0, None), (s1, None), (s2, None), (s3, None)],
        [(own, 0), (u, 0), (v, 0), (far, None)],
    )

    before, after_, across = [narrow_move(alone, 0, dz) for dz in (1, 3, 2)]
    swapped = narrow_move(both, 1, 0)
    ready = (before, after_, across, swapped)

    def far_blocks(part):
        return after(jnp.stack([t[part] for t in (after_, across, before)]), *ready)

    def pair_of(part):
        return after(jnp.stack([both[1, part], swapped[1, part]]), *ready)

    def x_blocks(first, rest):
        near = [(alone, None, 0, 0), (after_, None, 0, 1), (across, None, 0, 2), (before, None, 0, 3)]
        far = [(swapped, 0, 1, 0)] + [(rest, k, 1, k + 1) for k in range(3)]
        return [(a, lead, first if a is not rest else 0, *at_) for a, lead, *at_ in near + far]

    def z_blocks(first, pair, after_, before, near, far):
        blocks = [(near, None, 0, 0, 2), (far, None, 0, 1, 2)]
        for dz, source in ((0, pair), (1, after_), (3, before)):
            blocks += [(source, k, 0, k, dz) for k in range(2)]
        return blocks

    gu, hid = slice(0, 2), slice(2, 3)
    pair = pair_of(gu)
    z_before, z_after = narrow_move(pair, 0, 1), narrow_move(pair, 0, 3)
    rest = narrow_move(far_blocks(gu), 1, 0)
    near, far = narrow_move(z_before[0], 0, 1), narrow_move(z_after[1], 0, 3)
    blocks_x = x_blocks(0, rest)
    blocks_z = z_blocks(0, pair, z_after, z_before, near, far)

    pair = after(pair_of(hid), z_before, z_after)
    z_before, z_after = narrow_move(pair, 0, 1), narrow_move(pair, 0, 3)
    rest_hid = narrow_move(after(far_blocks(hid), rest), 1, 0)
    hid_near, hid_far = narrow_move(z_before[0], 0, 1), narrow_move(z_after[1], 0, 3)
    hid_x = x_blocks(2, rest_hid)
    hid_z = z_blocks(2, pair, z_after, z_before, hid_near, hid_far)

    keep, send = back(after(at, z_before, z_after), blocks_x, blocks_z, weights)
    from_core = wide_move(send, 0, 0, 1)
    grad_input = scatter_tokens(keep, from_core)

    grad_gate, grad_up = grads("grads", 2, after(at, from_core, hid_near, hid_far), blocks_x, blocks_z, 0, halves)
    (grad_down,) = grads("down", 1, after(at, grad_gate), hid_x, hid_z, 1, halves)
    return grad_input, grad_gate.T, grad_up.T, grad_down


def solution(mesh):
    return jax.shard_map(
        body,
        mesh=mesh,
        in_specs=(
            P("wide", "narrow"),
            P("wide", "narrow"),
            P("narrow", "wide"),
            P("narrow", "wide"),
            P("wide", "narrow"),
        ),
        out_specs=(
            P("wide", "narrow"),
            P("narrow", "wide"),
            P("narrow", "wide"),
            P("wide", "narrow"),
        ),
        check_vma=False,
    )
```

```python
import functools

import jax
import jax.numpy as jnp
from jax import lax
from jax.experimental import pallas as pl
from jax.experimental.pallas import tpu as pltpu
from jax.sharding import PartitionSpec as P

BF = jnp.bfloat16
F32 = jnp.float32
D = 1024
T = 1024
HALF = T // 2
B = 128
FF = 1848
RH = 928
R = RH // 2
N_BACK = 256
N_BLOCK = 512
VMEM = 32 * 1024 * 1024
VMEM_FAR = 44 * 1024 * 1024
VMEM_SUMS = 12 * 1024 * 1024

NT = (((1,), (1,)), ((), ()))
NN = (((1,), (0,)), ((), ()))
TN = (((0,), (0,)), ((), ()))


def dot(a, b, dims):
    return lax.dot_general(a, b, dims, preferred_element_type=F32)


def shape(*dims, dtype=BF):
    return jax.ShapeDtypeStruct(dims, dtype)


def params(limit=VMEM):
    return pltpu.CompilerParams(vmem_limit_bytes=limit)


def cost(flops, nbytes):
    return pl.CostEstimate(flops=int(flops), bytes_accessed=int(nbytes), transcendentals=0)


def narrow_move(value, dxh, dz):
    pairs = [
        (xh * 4 + z, ((xh + dxh) % 2) * 4 + (z + dz) % 4) for xh in range(2) for z in range(4)
    ]
    return lax.ppermute(value, "narrow", pairs)


def wide_move(value, dy, dxl, dc):
    pairs = [
        (y * 4 + xl * 2 + c, ((y + dy) % 4) * 4 + ((xl + dxl) % 2) * 2 + (c + dc) % 2)
        for y in range(4)
        for xl in range(2)
        for c in range(2)
    ]
    return lax.ppermute(value, "wide", pairs)


def first_kernel(which, slots, layout, n_outs, at, *refs):
    sources = sorted({w // 2 for w in which})
    own, other, *refs = refs
    weights, refs = refs[: len(which)], refs[len(which) :]
    outs, refs = refs[:n_outs], refs[n_outs:]
    *targets, sems = refs

    @pl.when(pl.program_id(0) == 0)
    def _():
        copies = []
        for s, (dxh, dz) in enumerate(slots):
            row = pl.ds(pl.multiple_of(lax.rem(at[1] + dz, 4) * B, B), B)
            for k, (source, target) in enumerate(zip(sources, targets)):
                place_, sem = target.at[s * B : (s + 1) * B, :], sems.at[k, s]
                near = pltpu.make_async_copy(own.at[source, row, :], place_, sem)
                far = pltpu.make_async_copy(other.at[source, row, :], place_, sem)
                pl.when(at[0] == dxh)(near.start)
                pl.when(at[0] != dxh)(far.start)
                copies.append(near)
        for copy in copies:
            copy.wait()

    for i, w in enumerate(which):
        res = dot(weights[i][...], targets[sources.index(w // 2)][...], NT).astype(BF)

        def store(outs):
            for out, members in zip(outs, layout):
                for k, s in enumerate(members):
                    value = res[:, s * B : (s + 1) * B]
                    if len(members) > 1:
                        out[k, i] = value
                    else:
                        out[i] = value

        if len(outs) == len(layout):
            store(outs)
        else:
            pl.when(pl.program_id(0) < 2)(functools.partial(store, outs[: len(layout)]))
            pl.when(pl.program_id(0) >= 2)(functools.partial(store, outs[len(layout) :]))


def rows_spec(array, lead=None, step=lambda r: r):
    if array.ndim == 3:
        return pl.BlockSpec((array.shape[0], R, B), lambda r, *_: (0, step(r), 0))
    if lead is None:
        return pl.BlockSpec((*array.shape[:2], R, B), lambda r, *_: (0, 0, step(r), 0))
    return pl.BlockSpec((1, array.shape[1], R, B), lambda r, *_: (lead, 0, step(r), 0))


def first(name, half, slots, layout, at, halves, weights):
    which = (0, 1, 2)
    n = len(which)
    base = 0 if half is None else 2 * half
    weight = pl.BlockSpec((R, D), lambda r, at: (base + r, 0))
    out_shape = [shape(len(m), n, RH, B) if len(m) > 1 else shape(n, RH, B) for m in layout]
    out_specs = [rows_spec(o) for o in out_shape]
    if half is None:
        out_specs = [rows_spec(o, step=lambda r: jnp.minimum(r, 1)) for o in out_shape]
        out_specs += [rows_spec(o, step=lambda r: jnp.maximum(r - 2, 0)) for o in out_shape]
        out_shape = out_shape * 2
    width = len(slots) * B
    steps = 4 if half is None else 2
    return pl.pallas_call(
        functools.partial(first_kernel, which, slots, layout, len(out_shape)),
        out_shape=out_shape,
        grid_spec=pltpu.PrefetchScalarGridSpec(
            num_scalar_prefetch=1,
            grid=(steps,),
            in_specs=[pl.BlockSpec(memory_space=pl.ANY)] * 2 + [weight] * n,
            out_specs=out_specs,
            scratch_shapes=[
                *[pltpu.VMEM((width, D), BF)] * 2,
                pltpu.SemaphoreType.DMA((2, len(slots))),
            ],
        ),
        compiler_params=params(VMEM_FAR if half is None else VMEM),
        cost_estimate=cost(n * 2 * steps * R * width * D, n * steps * R * (D + width) * 2),
        name=name,
    )(at, *halves, *[weights[w] for w in which])


def pick(group, lead, i):
    for ref in group:
        rank = len(ref.shape)
        n = ref.shape[rank - 3]
        if i < n:
            return (ref[lead, i] if rank == 4 else ref[i]).astype(F32)
        i -= n


def grouped(refs, sizes):
    refs = list(refs)
    return [[refs.pop(0) for _ in range(size)] for size in sizes]


def on_groups(name, kernel, groups, out_shape, leads=None):
    leads = leads or [None] * len(groups)
    sizes = [len(g) for g in groups]
    n = sum(sizes)
    arrays = [a for g in groups for a in g]

    def run(*refs):
        kernel(grouped(refs[:n], sizes), refs[n:])

    moved = sum(a.size for a in arrays) + sum(o.size for o in out_shape)
    return pl.pallas_call(
        run,
        out_shape=out_shape,
        grid=(2,),
        in_specs=[rows_spec(a, lead) for g, lead in zip(groups, leads) for a in g],
        out_specs=[rows_spec(o) for o in out_shape],
        compiler_params=params(VMEM_SUMS),
        cost_estimate=cost(moved, moved * 2),
        name=name,
    )(*arrays)


def x_sum(keep, recv, first_lead):
    one = recv.ndim == 3
    n = 1 if one else recv.shape[0]

    def kernel(groups, outs):
        for k, out in enumerate(outs):
            for i in range(3):
                out[i] = (pick(groups[0], first_lead + k, i) + pick(groups[1], k, i)).astype(BF)

    return on_groups(f"x_sum{n}", kernel, [(keep,), (recv,)], [shape(3, RH, B)] * n)


def z_mid(mid1, ra, mid3, rb):
    def kernel(groups, outs):
        for i in range(3):
            outs[0][0, i] = (pick(groups[0], 0, i) + pick(groups[1], 0, i)).astype(BF)
            outs[0][1, i] = pick(groups[0], 1, i).astype(BF)
            outs[1][0, i] = pick(groups[2], 0, i).astype(BF)
            outs[1][1, i] = (pick(groups[2], 1, i) + pick(groups[3], 1, i)).astype(BF)

    return on_groups("z_mid", kernel, [mid1, ra, mid3, rb], [shape(2, 3, RH, B)] * 2)


def z_far(own, u, v):
    def kernel(groups, outs):
        for i in range(3):
            total = pick(groups[0], 0, i) + pick(groups[1], 0, i) + pick(groups[2], 0, i)
            outs[0][i] = total.astype(BF)

    groups = [(own,), (u,), (v,)]
    return on_groups("z_far", kernel, groups, [shape(3, RH, B)], leads=[1, 1, 1])[0]


def swiglu(x_terms, z_terms):
    terms = [*x_terms, *z_terms]

    def kernel(groups, outs):
        alone, both = outs
        for k, mine in enumerate((groups[: len(x_terms)], groups[len(x_terms) :])):
            sums = []
            for i in range(3):
                acc = pick(mine[0], 0, i)
                for group in mine[1:]:
                    acc = acc + pick(group, 0, i)
                sums.append(acc)
            gate, up, grad = sums
            sig = jax.nn.sigmoid(gate)
            silu = gate * sig
            gate_grad = grad * up * sig * (1.0 + gate * (1.0 - sig))
            for i, value in enumerate((gate_grad, grad * silu, silu * up)):
                value = value.astype(BF)
                both[k, i] = value
                if k == 0:
                    alone[i] = value

    out_shape = [shape(3, RH, B), shape(2, 3, RH, B)]
    groups, leads = [(t,) for t, _ in terms], [lead for _, lead in terms]
    return on_groups("swiglu", kernel, groups, out_shape, leads=leads)


def distinct(blocks):
    arrays, places = [], []
    for array, lead, base, dxh, dz in blocks:
        for n, seen in enumerate(arrays):
            if seen is array:
                break
        else:
            n = len(arrays)
            arrays.append(array)
        places.append((n, lead, base, dxh, dz))
    return arrays, places


def place_copies(at, refs, places, targets, sems):
    copies = []
    for k, (n, lead, base, dxh, dz) in enumerate(places):
        column = (lax.rem(at[0] + dxh, 2) * 4 + lax.rem(at[1] + dz, 4)) * B
        part = pl.ds(pl.multiple_of(column, B), B)
        for i, target in enumerate(targets):
            source = refs[n].at[base + i] if lead is None else refs[n].at[lead, base + i]
            copies.append(pltpu.make_async_copy(source, target.at[:, part], sems.at[i, k]))
    return copies


def back_kernel(places, counts, at, *refs):
    refs = list(refs)
    arrays = [[refs.pop(0) for _ in range(count)] for count in counts]
    wg, wu, out_o, out_t, *acts, sems = refs
    halves = (slice(0, RH), slice(RH, 2 * RH))

    @pl.when(pl.program_id(0) == 0)
    def _():
        copies = []
        for half in range(2):
            targets = [act.at[halves[half], :] for act in acts]
            copies += place_copies(at, arrays[half], places[half], targets, sems.at[half])
        for copy in copies:
            copy.start()
        for copy in copies:
            copy.wait()
        last = slice(2 * RH - 16, 2 * RH)
        rows = lax.broadcasted_iota(jnp.int32, (16, T), 0) < FF - (2 * RH - 16)
        for act in acts:
            act[last, :] = jnp.where(rows, act[last, :], jnp.zeros((16, T), BF))

    rows = lax.broadcasted_iota(jnp.int32, (2 * RH, N_BACK), 0) < FF
    vg = jnp.where(rows, wg[...], jnp.zeros((2 * RH, N_BACK), BF))
    vu = jnp.where(rows, wu[...], jnp.zeros((2 * RH, N_BACK), BF))
    for k, out in enumerate((out_o, out_t)):
        part = slice(k * HALF, (k + 1) * HALF)
        total = dot(acts[0][:, part], vg, TN) + dot(acts[1][:, part], vu, TN)
        out[...] = total.astype(out.dtype)


def back(at, blocks_x, blocks_z, weights):
    (arrays_x, places_x), (arrays_z, places_z) = distinct(blocks_x), distinct(blocks_z)
    arrays = arrays_x + arrays_z
    weight = pl.BlockSpec((2 * RH, N_BACK), lambda n, at: (0, n))
    out = pl.BlockSpec((HALF, N_BACK), lambda n, at: (0, n))
    counts = (len(arrays_x), len(arrays_z))
    return pl.pallas_call(
        functools.partial(back_kernel, (places_x, places_z), counts),
        out_shape=[shape(HALF, D)] * 2,
        grid_spec=pltpu.PrefetchScalarGridSpec(
            num_scalar_prefetch=1,
            grid=(D // N_BACK,),
            in_specs=[pl.BlockSpec(memory_space=pl.ANY)] * len(arrays) + [weight] * 2,
            out_specs=[out] * 2,
            scratch_shapes=[pltpu.VMEM((2 * RH, T), BF)] * 2 + [pltpu.SemaphoreType.DMA((2, 2, 8))],
        ),
        compiler_params=params(),
        cost_estimate=cost(2 * 2 * FF * T * D, 2 * FF * (T + D) * 2 + T * D * 2),
        name="back",
    )(at, *arrays, *weights[:2])


def grads_kernel(places, counts, n, at, *refs):
    refs = list(refs)
    arrays = [[refs.pop(0) for _ in range(count)] for count in counts]
    own, other, *refs = refs
    outs, acts, tokens, sems = refs[:n], refs[n : 2 * n], refs[2 * n], refs[2 * n + 1]
    halves = (slice(0, RH), slice(RH, 2 * RH))
    copies = []
    for half in range(2):
        targets = [act.at[halves[half], :] for act in acts]
        copies.append(place_copies(at, arrays[half], places[half], targets, sems.at[half]))
    start = pl.program_id(0) == 0

    @pl.when(start)
    def _():
        for copy in copies[0] + copies[1]:
            copy.start()

    tokens[:HALF, :] = own[0]
    tokens[HALF:, :] = other[0]
    for half, rows in enumerate(halves):

        @pl.when(start)
        def _(half=half):
            for copy in copies[half]:
                copy.wait()

        for out, act in zip(outs, acts):
            out[rows, :] = dot(act[rows, :], tokens[...], NN).astype(BF)


def grads(name, n, at, blocks_x, blocks_z, k, halves):
    width = N_BACK if n > 1 else N_BLOCK
    (arrays_x, places_x), (arrays_z, places_z) = distinct(blocks_x), distinct(blocks_z)
    arrays = arrays_x + arrays_z
    token = pl.BlockSpec((1, HALF, width), lambda n, at: (k, 0, n))
    out = pl.BlockSpec((2 * RH, width), lambda n, at: (0, n))
    counts = (len(arrays_x), len(arrays_z))
    return pl.pallas_call(
        functools.partial(grads_kernel, (places_x, places_z), counts, n),
        out_shape=[shape(FF, D)] * n,
        grid_spec=pltpu.PrefetchScalarGridSpec(
            num_scalar_prefetch=1,
            grid=(D // width,),
            in_specs=[pl.BlockSpec(memory_space=pl.ANY)] * len(arrays) + [token] * 2,
            out_specs=[out] * n,
            scratch_shapes=[
                *[pltpu.VMEM((2 * RH, T), BF)] * n,
                pltpu.VMEM((T, width), BF),
                pltpu.SemaphoreType.DMA((2, n, 8)),
            ],
        ),
        compiler_params=params(),
        cost_estimate=cost(n * 2 * FF * T * D, n * FF * (T + D) * 2 + T * D * 2),
        name=name,
    )(at, *arrays, *halves)


def after(value, *earlier):
    return lax.optimization_barrier((value, *earlier))[0]


def scatter_tokens(keep, recv):
    total = keep.astype(F32) + recv.astype(F32)
    parts = [total[dy * B : (dy + 1) * B] for dy in range(4)]
    acc = parts[0]
    for dy in (1, 3, 2):
        acc = acc + wide_move(parts[dy].astype(BF), dy, 0, 0).astype(F32)
    far = wide_move(acc[B // 2 :].astype(BF), 0, 1, 0)
    return (acc[: B // 2] + far.astype(F32)).astype(BF)


def body(inputs, grad_out, w_gate, w_up, w_down):
    narrow = lax.axis_index("narrow")
    at = jnp.stack([narrow // 4, narrow % 4]).astype(jnp.int32)
    weights = (w_gate.T, w_up.T, w_down)
    wg, wu = weights[:2]

    pair = jnp.concatenate([inputs, wide_move(inputs, 0, 1, 0)])
    grads_y = jnp.stack([grad_out, *[wide_move(grad_out, -dy, 0, 0) for dy in (1, 2, 3)]])
    pairs = [pair, *[wide_move(pair, -dy, 0, 0) for dy in (1, 2, 3)]]
    grads_x = wide_move(grads_y, 0, 1, 0)
    pairs_g = jnp.stack([grads_y, grads_x], 1).reshape(HALF, D)
    tokens = jnp.stack([jnp.concatenate(pairs), pairs_g])
    halves = (tokens, wide_move(tokens, 0, 0, 1))

    keep2, send2, a2, b2 = first("far", None, ((0, 2), (1, 2)), ((0,), (1,)), at, halves, weights)
    recv2 = narrow_move(send2, 1, 0)
    ra, rb = narrow_move(a2, 0, 1), narrow_move(b2, 0, 3)
    (send,) = first("send", 0, ((1, 1), (1, 3)), ((0, 1),), after(at, a2), halves, weights)
    recv = narrow_move(send, 1, 0)
    mid_slots = ((0, 1), (1, 1), (0, 3), (1, 3))
    mid1, mid3 = first("mid", 1, mid_slots, ((0, 1), (2, 3)), after(at, send), halves, weights)
    u, v = z_mid((mid1,), (ra,), (mid3,), (rb,))
    u, v = after(u, recv2), after(v, recv2)
    u, v = narrow_move(u, 0, 1), narrow_move(v, 0, 3)
    (s2,) = x_sum(keep2, recv2, 0)
    s2 = narrow_move(s2, 0, 2)
    keep_slots = ((1, 0), (0, 0), (0, 1), (0, 3))
    send_0, keep = first("keep", 0, keep_slots, ((0,), (1, 2, 3)), after(at, mid1), halves, weights)
    recv_0 = narrow_move(send_0, 1, 0)
    (own,) = first("own", 1, ((0, 0), (1, 0)), ((0, 1),), after(at, keep), halves, weights)
    far = narrow_move(z_far(own, u, v), 1, 0)
    s1, s3 = x_sum(keep, recv, 1)
    s1, s3 = narrow_move(s1, 0, 1), narrow_move(s3, 0, 3)
    alone, both = swiglu(
        [(keep, 0), (recv_0, None), (s1, None), (s2, None), (s3, None)],
        [(own, 0), (u, 0), (v, 0), (far, None)],
    )

    before, after_, across = [narrow_move(alone, 0, dz) for dz in (1, 3, 2)]
    swapped = narrow_move(both, 1, 0)
    ready = (before, after_, across, swapped)

    def far_blocks(part):
        return after(jnp.stack([t[part] for t in (after_, across, before)]), *ready)

    def pair_of(part):
        return after(jnp.stack([both[1, part], swapped[1, part]]), *ready)

    def x_blocks(first, rest):
        near = [(alone, None, 0, 0), (after_, None, 0, 1), (across, None, 0, 2), (before, None, 0, 3)]
        far = [(swapped, 0, 1, 0)] + [(rest, k, 1, k + 1) for k in range(3)]
        return [(a, lead, first if a is not rest else 0, *at_) for a, lead, *at_ in near + far]

    def z_blocks(first, pair, after_, before, near, far):
        blocks = [(near, None, 0, 0, 2), (far, None, 0, 1, 2)]
        for dz, source in ((0, pair), (1, after_), (3, before)):
            blocks += [(source, k, 0, k, dz) for k in range(2)]
        return blocks

    gu, hid = slice(0, 2), slice(2, 3)
    pair = pair_of(gu)
    z_before, z_after = narrow_move(pair, 0, 1), narrow_move(pair, 0, 3)
    rest = narrow_move(far_blocks(gu), 1, 0)
    near, far = narrow_move(z_before[0], 0, 1), narrow_move(z_after[1], 0, 3)
    blocks_x = x_blocks(0, rest)
    blocks_z = z_blocks(0, pair, z_after, z_before, near, far)

    pair = after(pair_of(hid), z_before, z_after)
    z_before, z_after = narrow_move(pair, 0, 1), narrow_move(pair, 0, 3)
    rest_hid = narrow_move(after(far_blocks(hid), rest), 1, 0)
    hid_near, hid_far = narrow_move(z_before[0], 0, 1), narrow_move(z_after[1], 0, 3)
    hid_x = x_blocks(2, rest_hid)
    hid_z = z_blocks(2, pair, z_after, z_before, hid_near, hid_far)

    keep, send = back(after(at, z_before, z_after), blocks_x, blocks_z, weights)
    from_core = wide_move(send, 0, 0, 1)
    grad_input = scatter_tokens(keep, from_core)

    grad_gate, grad_up = grads("grads", 2, after(at, from_core, hid_near, hid_far), blocks_x, blocks_z, 0, halves)
    (grad_down,) = grads("down", 1, after(at, grad_gate), hid_x, hid_z, 1, halves)
    return grad_input, grad_gate.T, grad_up.T, grad_down


def solution(mesh):
    return jax.shard_map(
        body,
        mesh=mesh,
        in_specs=(
            P("wide", "narrow"),
            P("wide", "narrow"),
            P("narrow", "wide"),
            P("narrow", "wide"),
            P("wide", "narrow"),
        ),
        out_specs=(
            P("wide", "narrow"),
            P("narrow", "wide"),
            P("narrow", "wide"),
            P("wide", "narrow"),
        ),
        check_vma=False,
    )
```
